512 devices in a mesh: batch: 16 (over y, x), group: 32 (over z, core).
Axes of the slice: x: 4, y: 4, z: 16, core: 2. Of those that a mesh axis runs over, the one named last changes fastest.
Arguments:
- noise: bfloat16 [2048, 99840], P('batch', 'group'), may hold values from -24 to 24
- data: bfloat16 [2048, 99840], P('batch', 'group'), may hold values from -6 to 6
Outputs:
- targets: bfloat16 [2048, 99840], P('batch', 'group')
- potential: float32 [2048], replicated
The draws below stay inside these ranges and needn't reach their ends.
All inputs are finite; a program needn't handle non-finite values.
Results may differ from the reference program's by a relative error of at most 0.007.
Values may be sent and summed in bfloat16 or wider, within the bound.
A program may use at most 64 MiB of HBM per device.

```python
import jax
import jax.numpy as jnp
from jax import lax

ITERS = 4
FEAT = 99840
BATCH = 2048


def draw_noise(key, part):
    key = jax.random.fold_in(key, 11)
    row_key, value_key = jax.random.split(key, 2)
    picks = jax.random.randint(row_key, (BATCH,), 0, 8)
    rows_index = jnp.arange(BATCH)
    scaled = jnp.logical_or(picks == 0, rows_index == 0)
    factor = jnp.where(scaled, 4.0, 1.0).astype(jnp.float32)
    values = jnp.clip(jax.random.normal(value_key, (BATCH, FEAT), jnp.float32), -6.0, 6.0)
    return (values * factor[:, None]).astype(jnp.bfloat16)


def block_scale(stream_key, extent, pieces, least, largest):
    level = 1.0
    for dim, blocks in pieces:
        draws = jax.random.uniform(jax.random.fold_in(jax.random.fold_in(stream_key, 6), dim), (blocks,), jnp.float32, least / len(pieces), largest / len(pieces))
        level = level * jnp.repeat(jnp.exp(draws), extent[dim] // blocks).reshape((-1,) + (1,) * (len(extent) - 1 - dim))
    return level


def bell_draw(own_key, shape, scale, limit, cuts=(), held_as=jnp.bfloat16):
    gain = block_scale(own_key, shape, cuts, -0.22, 0.18) if cuts else 1.0
    drawn = jax.random.normal(own_key, shape, jnp.float32) * scale * gain
    return jnp.minimum(jnp.maximum(drawn, -limit), limit).astype(held_as)


def setup_inputs(seed: int = 0) -> dict:
    seeds = jax.random.split(jax.random.key(seed), 3)
    noise = draw_noise(jax.random.fold_in(seeds[2], 71), 0)
    data = bell_draw(seeds[1], (BATCH, FEAT), 1.0, 6.0, ((0, 16), (1, 32)))
    return {"noise": noise, "data": data}


def log_sum(values, axis):
    top = lax.optimization_barrier(jnp.max(values, axis=axis, keepdims=True))
    return jnp.squeeze(top, axis) + jnp.log(lax.optimization_barrier(jnp.sum(jnp.exp(values - top), axis=axis)))

def reference(noise, data):
    eps = 2.0 / jnp.sqrt(jnp.float32(FEAT))
    loga = -jnp.log(jnp.float32(BATCH))
    noise_sq = lax.optimization_barrier(jnp.sum(jnp.square(noise.astype(jnp.float32)), axis=1))
    data_sq = lax.optimization_barrier(jnp.sum(jnp.square(data.astype(jnp.float32)), axis=1))
    cross = jnp.dot(noise, data.T, preferred_element_type=jnp.float32)
    cost = (noise_sq[:, None] + data_sq[None, :] - 2.0 * cross) / jnp.float32(FEAT)
    potential = jnp.zeros((BATCH,), jnp.float32)
    for step in range(ITERS):
        rowpot = eps * loga - eps * log_sum((potential[None, :] - cost) / eps, 1)
        potential = eps * loga - eps * log_sum((rowpot[:, None] - cost) / eps, 0)
    scores = (potential[None, :] - cost) / eps
    weights = jnp.exp(scores - log_sum(scores, 1)[:, None]).astype(jnp.bfloat16)
    targets = jnp.dot(weights, data, preferred_element_type=jnp.float32).astype(jnp.bfloat16)
    return (targets, potential)
```

```python
import jax
import jax.numpy as jnp
import numpy as np
from jax import lax
from jax.experimental import pallas as pl
from jax.experimental.pallas import tpu as pltpu
from jax.sharding import PartitionSpec as P

MESH = pl.DeviceIdType.MESH
ITERS = 4
FEAT = 99840
BATCH = 2048
ROWS = 128
WIDE = 3120
PAD = 3200
TAIL = WIDE // 128 * 128
EPS = np.float32(2.0 / np.sqrt(np.float32(FEAT)))
LOGA = np.float32(-np.log(np.float32(BATCH)))
SCALE = np.float32(2.0 / (np.float64(FEAT) * np.float64(EPS)))
A_ROWS = 80
A_CUT = 48
N_SEM = 160
TILE = 640


def split3(value):
    high = value.astype(jnp.bfloat16).astype(jnp.float32)
    rest = value - high
    mid = rest.astype(jnp.bfloat16).astype(jnp.float32)
    return high, mid, rest - mid


def offset_of(s):
    return s + (s // 2) * (1 - 2 * (s % 2))


def pack(src_ref, store, own_parts, own_at, const, const_at):
    total = jnp.zeros((ROWS, 1), jnp.float32)
    for at in range(0, WIDE, 640):
        cut = slice(at, min(at + 640, WIDE))
        piece = src_ref[:, cut].astype(jnp.float32)
        total = total + jnp.sum(piece * piece, axis=1, keepdims=True)
    parts = split3(total * own_parts)
    lane = lax.broadcasted_iota(jnp.int32, (ROWS, PAD - TAIL), 1)
    extra = jnp.zeros((ROWS, PAD - TAIL), jnp.float32)
    for k, part in enumerate(parts):
        extra = jnp.where(lane == WIDE - TAIL + own_at + k, part, extra)
        extra = jnp.where(lane == WIDE - TAIL + const_at + k, jnp.float32(const), extra)
    store(extra.astype(jnp.bfloat16), lane)


def kernel(
    noise_ref, data_ref, out_ref, pot_ref,
    D, Nb, C, R0, R1, S1, R2, F, M, L, lbuf, pbuf, W, tail, send, recv,
):
    b = lax.axis_index("batch")
    g = lax.axis_index("group")
    y, x, z, c = b // 4, b % 4, g // 2, g % 2
    rho, s = z % 4, z // 4

    def dev(dy=0, dx=0, dz=0, dc=0):
        return (((y + dy) % 4) * 4 + (x + dx) % 4, ((z + dz) % 16) * 2 + (c + dc) % 2)

    right, left, up, down, sibling = dev(dx=1), dev(dx=3), dev(dy=1), dev(dy=3), dev(dc=1)
    count = [0]
    started = []

    def make(src, dst, device):
        k = count[0]
        count[0] += 1
        return pltpu.make_async_remote_copy(src, dst, send.at[k], recv.at[k], device_id=device, device_id_type=MESH)

    def go(src, dst, device):
        copy = make(src, dst, device)
        copy.start()
        started.append(copy)
        return copy

    near = [(dy, dx, 0, 0) for dy in range(4) for dx in range(4) if (dy, dx) != (0, 0)]
    far = [(0, 0, dz, 0) for dz in (1, 2, 14, 15)] + [(0, dx, dz, 0) for dx in range(4) for dz in (4, 8, 12)]
    peers = near + far + [(0, 0, 0, 1)]
    barrier = pltpu.get_barrier_semaphore()
    for peer in peers:
        pl.semaphore_signal(barrier, inc=1, device_id=dev(*peer), device_id_type=MESH)

    def rows(x_, y_, first=0, n=ROWS):
        return pl.ds(pl.multiple_of((x_ * 4 + y_) * ROWS + first, 16), n)

    def blk(x_, y_, first=0, n=ROWS):
        return D.at[rows(x_, y_, first, n)]

    own = rows(x, y)

    def place(ref, dst, where):
        dst[where, 0:TAIL] = ref[:, 0:TAIL]
        tail[:, 0 : WIDE - TAIL] = ref[:, TAIL:WIDE]

        def store(extra, lane):
            dst[where, TAIL:PAD] = jnp.where(lane < WIDE - TAIL, tail[...], extra)

        return store

    tail[...] = jnp.zeros_like(tail)
    pack(noise_ref, place(noise_ref, Nb, slice(0, ROWS)), -0.5, 0, -0.5, 3)
    pack(data_ref, place(data_ref, D, own), 1.0, 3, 1.0, 0)

    pl.semaphore_wait(barrier, len(peers))

    h = ROWS // 2

    def nb(i, first, n):
        return Nb.at[pl.ds(i * ROWS + first, n)]

    n_r0 = go(nb(0, 0, h), nb(2, 0, h), right)
    n_l0 = go(nb(0, h, h), nb(1, h, h), left)
    d_u0 = go(blk(x, y, 0, h), blk(x, y, 0, h), up)
    d_d0 = go(blk(x, y, h, h), blk(x, y, h, h), down)
    n_r1 = go(nb(0, h, h), nb(2, h, h), right)
    n_l1 = go(nb(0, 0, h), nb(1, 0, h), left)
    d_u1 = go(blk(x, y, h, h), blk(x, y, h, h), up)
    d_d1 = go(blk(x, y, 0, h), blk(x, y, 0, h), down)
    xr, xl, xo = (x + 1) % 4, (x + 3) % 4, (x + 2) % 4
    yu, yd, yo = (y + 1) % 4, (y + 3) % 4, (y + 2) % 4
    n_r0.wait_recv()
    n_ro = go(nb(2, 0, h), nb(3, 0, h), right)
    n_l0.wait_recv()
    n_lo = go(nb(1, h, h), nb(3, h, h), left)
    d_u0.wait_recv()
    d_uo = go(blk(x, yd, 0, h), blk(x, yd, 0, h), up)
    d_d0.wait_recv()
    d_do = go(blk(x, yu, h, h), blk(x, yu, h, h), down)

    nB = ROWS - A_ROWS
    a_r = go(blk(x, y, 0, A_ROWS), blk(x, y, 0, A_ROWS), right)
    a_l = go(blk(x, y, 0, A_ROWS), blk(x, y, 0, A_ROWS), left)
    b_r, b_l = {}, {}

    def send_b(table, y_name, y_, device):
        table[y_name] = go(blk(x, y_, A_ROWS, nB), blk(x, y_, A_ROWS, nB), device)

    def nt(a, b_):
        return lax.dot_general(a, b_, (((1,), (1,)), ((), ())), preferred_element_type=jnp.float32)

    def cols(y_):
        return pl.ds(pl.multiple_of(y_ * ROWS, ROWS), ROWS)

    n_r1.wait_recv()
    n_l1.wait_recv()
    C[0 : 3 * ROWS, cols(y)] = nt(Nb[0 : 3 * ROWS], D[own])
    d_u1.wait_recv()
    d_d1.wait_recv()
    send_b(b_r, "y", y, right)
    send_b(b_l, "d", yd, left)
    for y_ in (yu, yd):
        C[0 : 3 * ROWS, cols(y_)] = nt(Nb[0 : 3 * ROWS], D[rows(x, y_)])
    d_uo.wait_recv()
    d_do.wait_recv()
    C[0 : 3 * ROWS, cols(yo)] = nt(Nb[0 : 3 * ROWS], D[rows(x, yo)])
    n_ro.wait_recv()
    n_lo.wait_recv()
    C[3 * ROWS :, :] = nt(Nb[3 * ROWS :], D[pl.ds(pl.multiple_of(x * 4 * ROWS, ROWS), 4 * ROWS)])

    def half(core, i):
        return pl.ds(pl.multiple_of(i * ROWS + core * h, h), h)

    cores = [go(C.at[half(1 - c, i)], R0.at[pl.ds(i * h, h)], sibling) for i in range(4)]

    def sixteen(at):
        return pl.ds(pl.multiple_of(at, 16), 16)

    dz2 = 2 - 4 * c + 16
    steps = [(1, dev(dz=1)), (3, dev(dz=15)), (2, dev(dz=dz2))]
    window = {}
    for i in range(4):
        cores[i].wait_recv()
        R0[i * h : (i + 1) * h] = R0[i * h : (i + 1) * h] + C[half(c, i)]
        for t, (dq, device) in enumerate(steps):
            window[i, t] = go(
                R0.at[sixteen(i * h + 16 * ((rho + dq) % 4))], R1.at[t, pl.ds(i * 16, 16)], device
            )
    send_b(b_r, "u", yu, right)
    send_b(b_l, "o", yo, left)
    for i in range(4):
        for t in range(3):
            window[i, t].wait_recv()
        S1[i * 16 : (i + 1) * 16] = (
            R0[sixteen(i * h + 16 * rho)] + R1[0, i * 16 : (i + 1) * 16]
            + (R1[1, i * 16 : (i + 1) * 16] + R1[2, i * 16 : (i + 1) * 16])
        )
    stride = {}
    for d in (2, 1, 3):
        stride[d] = go(S1.at[sixteen(16 * ((s + d) % 4))], R2.at[d - 1], dev(dz=4 * d))

    a_r.wait_recv()
    a_l.wait_recv()
    ao_r = go(blk(xl, y, 0, A_CUT), blk(xl, y, 0, A_CUT), right)
    ao_l = go(blk(xr, y, A_CUT, A_ROWS - A_CUT), blk(xr, y, A_CUT, A_ROWS - A_CUT), left)
    send_b(b_r, "d", yd, right)
    send_b(b_l, "y", y, left)
    a_u, a_d = {}, {}

    def send_a(name, x_):
        a_u[name] = go(blk(x_, y, 0, A_ROWS), blk(x_, y, 0, A_ROWS), up)
        a_d[name] = go(blk(x_, y, 0, A_ROWS), blk(x_, y, 0, A_ROWS), down)

    send_a("r", xr)
    send_a("l", xl)

    for d in (1, 2, 3):
        stride[d].wait_recv()
    F[...] = (S1[sixteen(16 * s)] + R2[0] + (R2[1] + R2[2])) * SCALE

    mine = sixteen(c * h + 16 * rho)

    def part(x_):
        return M.at[mine, pl.ds(pl.multiple_of(x_ * 512, 512), 512)]

    dx = offset_of(s)
    home = {}
    for d in (2, 1, 3):
        home[d] = go(F, part(x), dev(dx=dx, dz=4 * d))
    home[0] = make(F, part(x), dev(dx=dx))

    @pl.when(s != 0)
    def _():
        home[0].start()

    @pl.when(s == 0)
    def _():
        M[mine, pl.ds(pl.multiple_of(x * 512, 512), 512)] = F[...]

    def fwd_b_r(name, y_):
        b_r[name].wait_recv()
        return go(blk(xl, y_, A_ROWS, nB), blk(xl, y_, A_ROWS, nB), right)

    def fwd_b_l(name, y_):
        b_l[name].wait_recv()
        return go(blk(xr, y_, A_ROWS, nB), blk(xr, y_, A_ROWS, nB), left)

    late = []
    spread, pair = {}, []
    for d in (0, 1, 3, 2):
        if d == 0:

            @pl.when(s != 0)
            def _():
                home[0].wait_recv()

        else:
            home[d].wait_recv()
        region = part((x + 4 - offset_of((s + 4 - d) % 4)) % 4)
        for t, (_, device) in enumerate(steps):
            spread[d, t] = go(region, region, device)
        pair.append(go(region, region, sibling))

    late.append(fwd_b_r("y", y))
    late.append(fwd_b_l("d", yd))
    send_b(b_r, "o", yo, right)
    send_b(b_l, "u", yu, left)
    ao_r.wait_recv()
    ao_l.wait_recv()
    send_a("o", xo)

    for t, dq in ((0, 3), (1, 1), (2, 2)):
        for d in range(4):
            spread[d, t].wait_recv()
        region = M.at[sixteen(c * h + 16 * ((rho + dq) % 4))]
        pair.append(go(region, region, sibling))
    for copy in pair:
        copy.wait_recv()

    def fwd_a(name, x_):
        a_u[name].wait_recv()
        late.append(go(blk(x_, yd, 0, A_CUT), blk(x_, yd, 0, A_CUT), up))
        a_d[name].wait_recv()
        late.append(go(blk(x_, yu, A_CUT, A_ROWS - A_CUT), blk(x_, yu, A_CUT, A_ROWS - A_CUT), down))

    def between(step):
        if step == 0:
            fwd_a("r", xr)
            late.append(fwd_b_r("u", yu))
        if step == 1:
            fwd_a("l", xl)
            late.append(fwd_b_l("o", yo))
        if step == 2:
            fwd_a("o", xo)

    def block(k):
        return M[:, k * ROWS : (k + 1) * ROWS]

    def row_lse():
        top = block(0) + pbuf[0:1, :]
        for k in range(1, 16):
            top = jnp.maximum(top, block(k) + pbuf[k : k + 1, :])
        top = jnp.max(top, axis=1, keepdims=True)
        total = jnp.exp(block(0) + pbuf[0:1, :] - top)
        for k in range(1, 16):
            total = total + jnp.exp(block(k) + pbuf[k : k + 1, :] - top)
        return top + jnp.log(jnp.sum(total, axis=1, keepdims=True))

    pbuf[...] = jnp.zeros_like(pbuf)
    for step in range(ITERS):
        rowpot = LOGA - row_lse()
        for k in range(16):
            values = block(k) + rowpot
            top = jnp.max(values, axis=0, keepdims=True)
            total = jnp.sum(jnp.exp(values - top), axis=0, keepdims=True)
            lbuf[step, k : k + 1, :] = top + jnp.log(total)
        slot = pl.ds(pl.multiple_of(b * 16, 16), 16)
        L[step, slot] = lbuf[step]
        swaps = [go(lbuf.at[step], L.at[step, slot], dev(*peer)) for peer in near]
        between(step)
        for copy in swaps:
            copy.wait_recv()
        top = L[step, 0:16]
        for k in range(1, 16):
            top = jnp.maximum(top, L[step, k * 16 : (k + 1) * 16])
        total = jnp.exp(L[step, 0:16] - top)
        for k in range(1, 16):
            total = total + jnp.exp(L[step, k * 16 : (k + 1) * 16] - top)
        pbuf[...] = LOGA - (top + jnp.log(total))

    lse = row_lse()
    for k in range(16):
        W[:, k * ROWS : (k + 1) * ROWS] = jnp.exp(block(k) + pbuf[k : k + 1, :] - lse).astype(jnp.bfloat16)
        pot_ref[(k % 4) * 4 + k // 4 : (k % 4) * 4 + k // 4 + 1, :] = pbuf[k : k + 1, :] * EPS

    for name in ("d", "o"):
        b_r[name].wait_recv()
    for name in ("y", "u"):
        b_l[name].wait_recv()
    for copy in late:
        copy.wait_recv()
    for at in range(0, WIDE, TILE):
        cut = slice(at, min(at + TILE, WIDE))
        out_ref[:, cut] = jnp.dot(W[...], D[:, cut], preferred_element_type=jnp.float32).astype(jnp.bfloat16)

    for copy in started:
        copy.wait_send()

    @pl.when(s != 0)
    def _():
        home[0].wait_send()


def local(noise, data):
    f32, bf16 = jnp.float32, jnp.bfloat16
    vmem = pl.BlockSpec(memory_space=pltpu.VMEM)
    targets, potential = pl.pallas_call(
        kernel,
        name="pairing",
        out_shape=(jax.ShapeDtypeStruct((ROWS, WIDE), bf16), jax.ShapeDtypeStruct((16, ROWS), f32)),
        in_specs=[vmem] * 2,
        out_specs=(vmem, vmem),
        scratch_shapes=[
            pltpu.VMEM((BATCH, PAD), bf16),
            pltpu.VMEM((4 * ROWS, PAD), bf16),
            pltpu.VMEM((512, 512), f32),
            pltpu.VMEM((256, 512), f32),
            pltpu.VMEM((3, 64, 512), f32),
            pltpu.VMEM((64, 512), f32),
            pltpu.VMEM((3, 16, 512), f32),
            pltpu.VMEM((16, 512), f32),
            pltpu.VMEM((ROWS, BATCH), f32),
            pltpu.VMEM((ITERS, 256, 128), f32),
            pltpu.VMEM((ITERS, 16, 128), f32),
            pltpu.VMEM((16, 128), f32),
            pltpu.VMEM((ROWS, BATCH), bf16),
            pltpu.VMEM((ROWS, PAD - TAIL), bf16),
            pltpu.SemaphoreType.DMA((N_SEM,)),
            pltpu.SemaphoreType.DMA((N_SEM,)),
        ],
        compiler_params=pltpu.CompilerParams(
            collective_id=0, has_side_effects=True, vmem_limit_bytes=48 * 1024 * 1024
        ),
    )(noise, data)
    return targets, potential.reshape(BATCH)


def solution(mesh):
    in_specs = (P("batch", "group"), P("batch", "group"))
    out_specs = (P("batch", "group"), P())
    return jax.shard_map(local, mesh=mesh, in_specs=in_specs, out_specs=out_specs, check_vma=False)
```

```python
import jax
import jax.numpy as jnp
import numpy as np
from jax import lax
from jax.experimental import pallas as pl
from jax.experimental.pallas import tpu as pltpu
from jax.sharding import PartitionSpec as P

MESH = pl.DeviceIdType.MESH
ITERS = 4
FEAT = 99840
BATCH = 2048
ROWS = 128
WIDE = 3120
DEEP = WIDE + 16
EPS = np.float32(2.0 / np.sqrt(np.float32(FEAT)))
LOGA = np.float32(-np.log(np.float32(BATCH)))
SCALE = np.float32(2.0 / (np.float64(FEAT) * np.float64(EPS)))
A = ((0, 784), (784, 1168))
A_DEEP = 1952
B = ((1952, 400), (2352, 400), (2752, 384))
HALF = 1536
N_SEM = 224
TILE = 624


def split3(value):
    high = value.astype(jnp.bfloat16).astype(jnp.float32)
    rest = value - high
    mid = rest.astype(jnp.bfloat16).astype(jnp.float32)
    return high, mid, rest - mid


def offset_of(s):
    return s + (s // 2) * (1 - 2 * (s % 2))


def place(src_ref, dst, start, factor, own_at, const, const_at):
    def chunk(k, total):
        at = pl.multiple_of(k * 240, 16)
        piece = src_ref[pl.ds(at, 240)]
        dst[pl.ds(pl.multiple_of(start + at, 16), 240)] = piece
        piece = piece.astype(jnp.float32)
        return total + jnp.sum((piece * piece).reshape(30, 8, ROWS), axis=0)

    total = lax.fori_loop(0, WIDE // 240, chunk, jnp.zeros((8, ROWS), jnp.float32))
    parts = split3(jnp.sum(total, axis=0, keepdims=True) * factor)
    line = lax.broadcasted_iota(jnp.int32, (16, ROWS), 0)
    extra = jnp.zeros((16, ROWS), jnp.float32)
    for k, part in enumerate(parts):
        extra = jnp.where(line == own_at + k, part, extra)
        extra = jnp.where(line == const_at + k, jnp.float32(const), extra)
    dst[pl.ds(pl.multiple_of(start + WIDE, 16), 16)] = extra.astype(jnp.bfloat16)


def kernel(
    noise_ref, data_ref, out_ref, pot_ref,
    D, NT, Nr, C, R0, R1, S1, R2, F, M, L, lbuf, pbuf, W, known, send, recv,
):
    b = lax.axis_index("batch")
    g = lax.axis_index("group")
    y, x, z, c = b // 4, b % 4, g // 2, g % 2
    rho, s = z % 4, z // 4

    def dev(dy=0, dx=0, dz=0, dc=0):
        return (((y + dy) % 4) * 4 + (x + dx) % 4, ((z + dz) % 16) * 2 + (c + dc) % 2)

    right, left, up, down, sibling = dev(dx=1), dev(dx=3), dev(dy=1), dev(dy=3), dev(dc=1)
    count = [0]
    started = []

    def make(src, dst, device):
        k = count[0]
        count[0] += 1
        assert k < N_SEM
        return pltpu.make_async_remote_copy(src, dst, send.at[k], recv.at[k], device_id=device, device_id_type=MESH)

    def go(src, dst, device):
        copy = make(src, dst, device)
        copy.start()
        started.append(copy)
        return copy

    barrier = pltpu.get_barrier_semaphore()
    next_ones = (right, left, up, down, dev(dz=1), dev(dz=15), sibling)
    for device in next_ones:
        pl.semaphore_signal(barrier, inc=1, device_id=device, device_id_type=MESH)

    def tell(k, *devices):
        for device in devices:
            pl.semaphore_signal(known.at[k], inc=1, device_id=device, device_id_type=MESH)

    def hear(k, n=1):
        pl.semaphore_wait(known.at[k], n)

    def rows(x_, y_, first=0, n=DEEP):
        return pl.ds(pl.multiple_of((x_ * 4 + y_) * DEEP + first, 16), n)

    def blk(x_, y_, first=0, n=DEEP):
        return D.at[rows(x_, y_, first, n)]

    def nb(i, first, n):
        return NT.at[pl.ds(i * DEEP + first, n)]

    place(noise_ref, NT, 0, -0.5, 0, -0.5, 3)
    place(data_ref, D, (x * 4 + y) * DEEP, 1.0, 3, 1.0, 0)
    pl.semaphore_wait(barrier, len(next_ones))

    one, two = (0, HALF), (HALF, DEEP - HALF)
    n_r0 = go(nb(0, *one), nb(2, *one), right)
    n_l0 = go(nb(0, *two), nb(1, *two), left)
    d_u0 = go(blk(x, y, *one), blk(x, y, *one), up)
    d_d0 = go(blk(x, y, *two), blk(x, y, *two), down)
    n_r1 = go(nb(0, *two), nb(2, *two), right)
    n_l1 = go(nb(0, *one), nb(1, *one), left)
    d_u1 = go(blk(x, y, *two), blk(x, y, *two), up)
    d_d1 = go(blk(x, y, *one), blk(x, y, *one), down)
    xr, xl, xo = (x + 1) % 4, (x + 3) % 4, (x + 2) % 4
    yu, yd, yo = (y + 1) % 4, (y + 3) % 4, (y + 2) % 4
    tell(0, right)
    tell(1, up)
    tell(2, dev(dz=1))
    tell(3, dev(dz=15))

    def flip(i, part):
        first, n = part
        for at in range(first, first + n, ROWS):
            size = min(ROWS, first + n - at)
            Nr[i * ROWS : (i + 1) * ROWS, at : at + size] = NT[i * DEEP + at : i * DEEP + at + size, :].T

    flip(0, (0, DEEP))
    for k in range(4):
        hear(k)
    tell(4, dev(dz=2))
    tell(5, dev(dz=14))
    tell(6, up, down, dev(dy=2))
    n_r0.wait_recv()
    n_ro = go(nb(2, *one), nb(3, *one), right)
    n_l0.wait_recv()
    n_lo = go(nb(1, *two), nb(3, *two), left)
    d_u0.wait_recv()
    d_uo = go(blk(x, yd, *one), blk(x, yd, *one), up)
    d_d0.wait_recv()
    d_do = go(blk(x, yu, *two), blk(x, yu, *two), down)
    flip(2, one)
    flip(1, two)
    hear(4)
    hear(5)
    hear(6, 3)
    tell(7, dev(dz=4))

    a_r, a_l = {}, {}
    for piece in A:
        a_r[piece] = go(blk(x, y, *piece), blk(x, y, *piece), right)
        a_l[piece] = go(blk(x, y, *piece), blk(x, y, *piece), left)
    b_r, b_l = {}, {}

    def send_b(r_name, r_y, l_name, l_y, *pieces):
        for piece in pieces:
            b_r[r_name, piece] = go(blk(x, r_y, *piece), blk(x, r_y, *piece), right)
            b_l[l_name, piece] = go(blk(x, l_y, *piece), blk(x, l_y, *piece), left)

    a_u, a_d = {}, {}

    def send_a(name, x_, piece):
        a_u[name, piece] = go(blk(x_, y, *piece), blk(x_, y, *piece), up)
        a_d[name, piece] = go(blk(x_, y, *piece), blk(x_, y, *piece), down)

    def turn_a(piece):
        a_r[piece].wait_recv()
        a_l[piece].wait_recv()
        send_a("r", xr, piece)
        send_a("l", xl, piece)

    late = []

    def fwd_b(r_name, r_y, l_name, l_y, *pieces):
        for piece in pieces:
            b_r.pop((r_name, piece)).wait_recv()
            late.append(go(blk(xl, r_y, *piece), blk(xl, r_y, *piece), right))
            b_l.pop((l_name, piece)).wait_recv()
            late.append(go(blk(xr, l_y, *piece), blk(xr, l_y, *piece), left))

    def fwd_a(name, x_, piece):
        first, size = piece
        n = size // 32 * 16
        a_u[name, piece].wait_recv()
        late.append(go(blk(x_, yd, first, n), blk(x_, yd, first, n), up))
        a_d[name, piece].wait_recv()
        late.append(go(blk(x_, yu, first + n, size - n), blk(x_, yu, first + n, size - n), down))

    def cross(i, n, j, y_):
        C[i * ROWS : (i + n) * ROWS, j * ROWS : (j + 1) * ROWS] = jnp.dot(
            Nr[i * ROWS : (i + n) * ROWS, :], D[rows(x, y_)], preferred_element_type=jnp.float32
        )

    h = ROWS // 2

    def half(core, i):
        return pl.ds(pl.multiple_of(i * ROWS + core * h, h), h)

    def sixteen(at):
        return pl.ds(pl.multiple_of(at, 16), 16)

    steps = [(1, dev(dz=1)), (3, dev(dz=15)), (2, dev(dz=18 - 4 * c))]

    def to_core(blocks):
        copies = []
        for i, first, n, at in blocks:
            copy = go(C.at[half(1 - c, i), pl.ds(first, n)], R0.at[:, pl.ds(at, n)], sibling)
            copies.append((copy, half(c, i), first, n, at))
        return copies

    def to_window(copies, at, n):
        for copy, mine_, first, size, to in copies:
            copy.wait_recv()
            R0[:, to : to + size] = R0[:, to : to + size] + C[mine_, first : first + size]
        return [
            go(R0.at[sixteen(16 * ((rho + dq) % 4)), pl.ds(at, n)], R1.at[t, :, pl.ds(at, n)], device)
            for t, (dq, device) in enumerate(steps)
        ]

    def add_window(copies, blocks):
        for copy in copies:
            copy.wait_recv()
        for i, first, n, at in blocks:
            for k in range(0, n, ROWS):
                cut = slice(at + k, at + k + ROWS)
                y_ = (y, yu, yd, yo)[(first + k) // ROWS]
                S1[i * 16 : (i + 1) * 16, pl.ds(pl.multiple_of(y_ * ROWS, ROWS), ROWS)] = (
                    R0[sixteen(16 * rho), cut] + R1[0, :, cut] + (R1[1, :, cut] + R1[2, :, cut])
                )

    early = [(0, 0, 384, 0), (1, 0, 384, 384), (2, 0, 384, 768)]
    rest = [(0, 384, 128, 1152), (1, 384, 128, 1280), (2, 384, 128, 1408), (3, 0, 512, 1536)]

    n_r1.wait_recv()
    flip(2, two)
    n_l1.wait_recv()
    flip(1, one)
    cross(0, 3, 0, y)
    d_u1.wait_recv()
    d_d1.wait_recv()
    send_b("y", y, "d", yd, *B)
    cross(0, 3, 1, yu)
    cross(0, 3, 2, yd)
    early_core = to_core(early)
    early_window = to_window(early_core, 0, 1152)
    hear(7)
    tell(8, dev(dz=4), dev(dz=8), dev(dz=12))
    d_uo.wait_recv()
    d_do.wait_recv()
    cross(0, 3, 3, yo)
    n_ro.wait_recv()
    flip(3, one)
    n_lo.wait_recv()
    flip(3, two)
    for j, y_ in enumerate((y, yu, yd, yo)):
        cross(3, 1, j, y_)
    rest_core = to_core(rest)
    add_window(early_window, early)
    rest_window = to_window(rest_core, 1152, 896)
    turn_a(A[0])
    add_window(rest_window, rest)
    stride = {}
    for d in (2, 1, 3):
        stride[d] = go(S1.at[sixteen(16 * ((s + d) % 4))], R2.at[d - 1], dev(dz=4 * d))
    turn_a(A[1])
    ao_r = go(blk(xl, y, 0, A_DEEP // 2), blk(xl, y, 0, A_DEEP // 2), right)
    ao_l = go(blk(xr, y, A_DEEP // 2, A_DEEP // 2), blk(xr, y, A_DEEP // 2, A_DEEP // 2), left)
    hear(8, 3)
    for d in (1, 2, 3):
        stride[d].wait_recv()
    F[...] = (S1[sixteen(16 * s)] + R2[0] + (R2[1] + R2[2])) * SCALE

    mine = sixteen(c * h + 16 * rho)

    def part(x_):
        return M.at[mine, pl.ds(pl.multiple_of(x_ * 512, 512), 512)]

    dx = offset_of(s)
    home = {}
    for d in (2, 1, 3):
        home[d] = go(F, part(x), dev(dx=dx, dz=4 * d))
    home[0] = make(F, part(x), dev(dx=dx))

    @pl.when(s != 0)
    def _():
        home[0].start()

    @pl.when(s == 0)
    def _():
        M[mine, pl.ds(pl.multiple_of(x * 512, 512), 512)] = F[...]

    fwd_a("r", xr, A[0])
    fwd_a("l", xl, A[0])
    send_b("u", yu, "o", yo, *B)
    fwd_b("y", y, "d", yd, *B)
    spread, pair = {}, []
    for d in (0, 1, 3, 2):
        if d == 0:

            @pl.when(s != 0)
            def _():
                home[0].wait_recv()

        else:
            home[d].wait_recv()
        region = part((x + 4 - offset_of((s + 4 - d) % 4)) % 4)
        for t, (_, device) in enumerate(steps):
            spread[d, t] = go(region, region, device)
        pair.append(go(region, region, sibling))

    send_b("d", yd, "y", y, B[0])
    ao_r.wait_recv()
    ao_l.wait_recv()
    for piece in A:
        send_a("o", xo, piece)

    for t, dq in ((0, 3), (1, 1), (2, 2)):
        for d in range(4):
            spread[d, t].wait_recv()
        region = M.at[sixteen(c * h + 16 * ((rho + dq) % 4))]
        pair.append(go(region, region, sibling))
    for copy in pair:
        copy.wait_recv()

    def between(step):
        if step == 0:
            fwd_a("r", xr, A[1])
            send_b("d", yd, "y", y, *B[1:])
        if step == 1:
            fwd_a("l", xl, A[1])
            send_b("o", yo, "u", yu, *B[:2])
        if step == 2:
            fwd_a("o", xo, A[0])
            send_b("o", yo, "u", yu, B[2])
            fwd_b("u", yu, "o", yo, B[0])
        if step == 3:
            fwd_a("o", xo, A[1])
            fwd_b("u", yu, "o", yo, *B[1:])

    def block(k):
        return M[:, k * ROWS : (k + 1) * ROWS]

    def row_lse():
        top = block(0) + pbuf[0:1, :]
        for k in range(1, 16):
            top = jnp.maximum(top, block(k) + pbuf[k : k + 1, :])
        top = jnp.max(top, axis=1, keepdims=True)
        total = jnp.exp(block(0) + pbuf[0:1, :] - top)
        for k in range(1, 16):
            total = total + jnp.exp(block(k) + pbuf[k : k + 1, :] - top)
        return top + jnp.log(jnp.sum(total, axis=1, keepdims=True))

    near = [(dy, dx, 0, 0) for dy in range(4) for dx in range(4) if (dy, dx) != (0, 0)]
    near.sort(key=lambda peer: -min(peer[0], 4 - peer[0]) - min(peer[1], 4 - peer[1]))
    pbuf[...] = jnp.zeros_like(pbuf)
    for step in range(ITERS):
        rowpot = LOGA - row_lse()
        for k in range(16):
            values = block(k) + rowpot
            top = jnp.max(values, axis=0, keepdims=True)
            total = jnp.sum(jnp.exp(values - top), axis=0, keepdims=True)
            lbuf[step, k : k + 1, :] = top + jnp.log(total)
        slot = pl.ds(pl.multiple_of(b * 16, 16), 16)
        L[step, slot] = lbuf[step]
        swaps = [go(lbuf.at[step], L.at[step, slot], dev(*peer)) for peer in near]
        between(step)
        for copy in swaps:
            copy.wait_recv()
        top = L[step, 0:16]
        for k in range(1, 16):
            top = jnp.maximum(top, L[step, k * 16 : (k + 1) * 16])
        total = jnp.exp(L[step, 0:16] - top)
        for k in range(1, 16):
            total = total + jnp.exp(L[step, k * 16 : (k + 1) * 16] - top)
        pbuf[...] = LOGA - (top + jnp.log(total))

    lse = row_lse()
    for k in range(16):
        W[:, k * ROWS : (k + 1) * ROWS] = jnp.exp(block(k) + pbuf[k : k + 1, :] - lse).astype(jnp.bfloat16)
        pot_ref[(k % 4) * 4 + k // 4 : (k % 4) * 4 + k // 4 + 1, :] = pbuf[k : k + 1, :] * EPS

    for copy in [*b_r.values(), *b_l.values(), *late]:
        copy.wait_recv()
    for at in range(0, WIDE, TILE):
        all_rows = jnp.concatenate([D[k * DEEP + at : k * DEEP + at + TILE, :] for k in range(16)], axis=1)
        out_ref[at : at + TILE, :] = lax.dot_general(
            all_rows, W[...], (((1,), (1,)), ((), ())), preferred_element_type=jnp.float32
        ).astype(jnp.bfloat16)

    for copy in started:
        copy.wait_send()

    @pl.when(s != 0)
    def _():
        home[0].wait_send()


def local(noise, data):
    f32, bf16 = jnp.float32, jnp.bfloat16
    vmem = pl.BlockSpec(memory_space=pltpu.VMEM)
    targets, potential = pl.pallas_call(
        kernel,
        name="pairing",
        out_shape=(jax.ShapeDtypeStruct((WIDE, ROWS), bf16), jax.ShapeDtypeStruct((16, ROWS), f32)),
        in_specs=[vmem] * 2,
        out_specs=(vmem, vmem),
        scratch_shapes=[
            pltpu.VMEM((16 * DEEP, ROWS), bf16),
            pltpu.VMEM((4 * DEEP, ROWS), bf16),
            pltpu.VMEM((4 * ROWS, DEEP), bf16),
            pltpu.VMEM((512, 512), f32),
            pltpu.VMEM((64, 2048), f32),
            pltpu.VMEM((3, 16, 2048), f32),
            pltpu.VMEM((64, 512), f32),
            pltpu.VMEM((3, 16, 512), f32),
            pltpu.VMEM((16, 512), f32),
            pltpu.VMEM((ROWS, BATCH), f32),
            pltpu.VMEM((ITERS, 256, 128), f32),
            pltpu.VMEM((ITERS, 16, 128), f32),
            pltpu.VMEM((16, 128), f32),
            pltpu.VMEM((ROWS, BATCH), bf16),
            pltpu.SemaphoreType.REGULAR((9,)),
            pltpu.SemaphoreType.DMA((N_SEM,)),
            pltpu.SemaphoreType.DMA((N_SEM,)),
        ],
        compiler_params=pltpu.CompilerParams(
            collective_id=0, has_side_effects=True, vmem_limit_bytes=48 * 1024 * 1024
        ),
    )(noise.T, data.T)
    return targets.T, potential.reshape(BATCH)


def solution(mesh):
    in_specs = (P("batch", "group"), P("batch", "group"))
    out_specs = (P("batch", "group"), P())
    return jax.shard_map(local, mesh=mesh, in_specs=in_specs, out_specs=out_specs, check_vma=False)
```

```python
import jax
import jax.numpy as jnp
import numpy as np
from jax import lax
from jax.experimental import pallas as pl
from jax.experimental.pallas import tpu as pltpu
from jax.sharding import PartitionSpec as P

MESH = pl.DeviceIdType.MESH
ITERS = 4
FEAT = 99840
BATCH = 2048
ROWS = 128
WIDE = 3120
DEEP = WIDE + 16
EPS = np.float32(2.0 / np.sqrt(np.float32(FEAT)))
LOGA = np.float32(-np.log(np.float32(BATCH)))
SCALE = np.float32(2.0 / (np.float64(FEAT) * np.float64(EPS)))
A = ((0, 784), (784, 1168))
AO = ((0, 656), (656, 656), (1312, 640))
A_DEEP = 1952
B = ((1952, 400), (2352, 400), (2752, 384))
HALF = 1536
N_SEM = 224
TILE = 624


def split3(value):
    high = value.astype(jnp.bfloat16).astype(jnp.float32)
    rest = value - high
    mid = rest.astype(jnp.bfloat16).astype(jnp.float32)
    return high, mid, rest - mid


def offset_of(s):
    return s + (s // 2) * (1 - 2 * (s % 2))


def place(dst, start, factor, own_at, const, const_at):
    def chunk(k, total):
        at = pl.multiple_of(k * 240, 16)
        piece = dst[pl.ds(pl.multiple_of(start + at, 16), 240)].astype(jnp.float32)
        return total + jnp.sum((piece * piece).reshape(30, 8, ROWS), axis=0)

    total = lax.fori_loop(0, WIDE // 240, chunk, jnp.zeros((8, ROWS), jnp.float32))
    parts = split3(jnp.sum(total, axis=0, keepdims=True) * factor)
    line = lax.broadcasted_iota(jnp.int32, (16, ROWS), 0)
    extra = jnp.zeros((16, ROWS), jnp.float32)
    for k, part in enumerate(parts):
        extra = jnp.where(line == own_at + k, part, extra)
        extra = jnp.where(line == const_at + k, jnp.float32(const), extra)
    dst[pl.ds(pl.multiple_of(start + WIDE, 16), 16)] = extra.astype(jnp.bfloat16)


def kernel(
    noise_ref, data_ref, out_ref, pot_ref,
    D, NT, Nr, C, R0, R1, S1, R2, F, M, L, lbuf, pbuf, W, known, load, send, recv,
):
    b = lax.axis_index("batch")
    g = lax.axis_index("group")
    y, x, z, c = b // 4, b % 4, g // 2, g % 2
    rho, s = (z + 2) % 4, z // 4
    hops = (6, 10, 2, 14)

    def dev(dy=0, dx=0, dz=0, dc=0):
        return (((y + dy) % 4) * 4 + (x + dx) % 4, ((z + dz) % 16) * 2 + (c + dc) % 2)

    right, left, up, down, sibling = dev(dx=1), dev(dx=3), dev(dy=1), dev(dy=3), dev(dc=1)
    count = [0]
    started = []

    def make(src, dst, device):
        k = count[0]
        count[0] += 1
        assert k < N_SEM
        return pltpu.make_async_remote_copy(src, dst, send.at[k], recv.at[k], device_id=device, device_id_type=MESH)

    def go(src, dst, device):
        copy = make(src, dst, device)
        copy.start()
        started.append(copy)
        return copy

    own = (x * 4 + y) * DEEP
    loads = [
        pltpu.make_async_copy(noise_ref, NT.at[pl.ds(0, WIDE)], load.at[0]),
        pltpu.make_async_copy(data_ref, D.at[pl.ds(pl.multiple_of(own, 16), WIDE)], load.at[1]),
    ]
    for copy in loads:
        copy.start()

    barrier = pltpu.get_barrier_semaphore()
    next_ones = (right, left, up, down, dev(dz=1), dev(dz=15), sibling)
    for device in next_ones:
        pl.semaphore_signal(barrier, inc=1, device_id=device, device_id_type=MESH)

    def tell(k, *devices):
        for device in devices:
            pl.semaphore_signal(known.at[k], inc=1, device_id=device, device_id_type=MESH)

    def hear(k, n=1):
        pl.semaphore_wait(known.at[k], n)

    def rows(x_, y_, first=0, n=DEEP):
        return pl.ds(pl.multiple_of((x_ * 4 + y_) * DEEP + first, 16), n)

    def blk(x_, y_, first=0, n=DEEP):
        return D.at[rows(x_, y_, first, n)]

    def nb(i, first, n):
        return NT.at[pl.ds(i * DEEP + first, n)]

    loads[0].wait()
    place(NT, 0, -0.5, 0, -0.5, 3)
    loads[1].wait()
    place(D, own, 1.0, 3, 1.0, 0)
    pl.semaphore_wait(barrier, len(next_ones))

    one, two = (0, HALF), (HALF, DEEP - HALF)
    n_r0 = go(nb(0, *one), nb(2, *one), right)
    n_l0 = go(nb(0, *two), nb(1, *two), left)
    d_u0 = go(blk(x, y, *one), blk(x, y, *one), up)
    d_d0 = go(blk(x, y, *two), blk(x, y, *two), down)
    n_r1 = go(nb(0, *two), nb(2, *two), right)
    n_l1 = go(nb(0, *one), nb(1, *one), left)
    d_u1 = go(blk(x, y, *two), blk(x, y, *two), up)
    d_d1 = go(blk(x, y, *one), blk(x, y, *one), down)
    xr, xl, xo = (x + 1) % 4, (x + 3) % 4, (x + 2) % 4
    yu, yd, yo = (y + 1) % 4, (y + 3) % 4, (y + 2) % 4
    tell(0, right)
    tell(1, up)
    tell(2, dev(dz=1))
    tell(3, dev(dz=15))

    def flip(i, part):
        first, n = part
        for at in range(first, first + n, ROWS):
            size = min(ROWS, first + n - at)
            Nr[i * ROWS : (i + 1) * ROWS, at : at + size] = NT[i * DEEP + at : i * DEEP + at + size, :].T

    flip(0, (0, DEEP))
    for k in range(4):
        hear(k)
    tell(4, dev(dz=2))
    tell(5, dev(dz=14))
    tell(6, up, down, dev(dy=2))
    n_r0.wait_recv()
    n_ro = go(nb(2, *one), nb(3, *one), right)
    n_l0.wait_recv()
    n_lo = go(nb(1, *two), nb(3, *two), left)
    d_u0.wait_recv()
    d_uo = go(blk(x, yd, *one), blk(x, yd, *one), up)
    d_d0.wait_recv()
    d_do = go(blk(x, yu, *two), blk(x, yu, *two), down)
    flip(2, one)
    flip(1, two)
    hear(4)
    hear(5)
    hear(6, 3)
    tell(7, dev(dz=2))
    tell(8, dev(dz=14))

    a_r, a_l = {}, {}
    for piece in A:
        a_r[piece] = go(blk(x, y, *piece), blk(x, y, *piece), right)
        a_l[piece] = go(blk(x, y, *piece), blk(x, y, *piece), left)
    b_r, b_l = {}, {}

    def send_b(r_name, r_y, l_name, l_y, *pieces):
        for piece in pieces:
            b_r[r_name, piece] = go(blk(x, r_y, *piece), blk(x, r_y, *piece), right)
            b_l[l_name, piece] = go(blk(x, l_y, *piece), blk(x, l_y, *piece), left)

    a_u, a_d = {}, {}

    def send_a(name, x_, piece):
        a_u[name, piece] = go(blk(x_, y, *piece), blk(x_, y, *piece), up)
        a_d[name, piece] = go(blk(x_, y, *piece), blk(x_, y, *piece), down)

    def turn_a(piece):
        a_r[piece].wait_recv()
        a_l[piece].wait_recv()
        send_a("r", xr, piece)
        send_a("l", xl, piece)

    late = []

    def fwd_b(r_name, r_y, l_name, l_y, *pieces):
        for piece in pieces:
            b_r.pop((r_name, piece)).wait_recv()
            late.append(go(blk(xl, r_y, *piece), blk(xl, r_y, *piece), right))
            b_l.pop((l_name, piece)).wait_recv()
            late.append(go(blk(xr, l_y, *piece), blk(xr, l_y, *piece), left))

    def fwd_a(name, x_, piece):
        first, size = piece
        n = size // 32 * 16
        a_u[name, piece].wait_recv()
        late.append(go(blk(x_, yd, first, n), blk(x_, yd, first, n), up))
        a_d[name, piece].wait_recv()
        late.append(go(blk(x_, yu, first + n, size - n), blk(x_, yu, first + n, size - n), down))

    def cross(i, n, j, y_):
        C[i * ROWS : (i + n) * ROWS, j * ROWS : (j + 1) * ROWS] = jnp.dot(
            Nr[i * ROWS : (i + n) * ROWS, :], D[rows(x, y_)], preferred_element_type=jnp.float32
        )

    h = ROWS // 2

    def half(core, i):
        return pl.ds(pl.multiple_of(i * ROWS + core * h, h), h)

    def sixteen(at):
        return pl.ds(pl.multiple_of(at, 16), 16)

    steps = [(1, dev(dz=1)), (3, dev(dz=15)), (2, dev(dz=18 - 4 * c))]

    def to_core(blocks):
        copies = []
        for i, first, n, at in blocks:
            copy = go(C.at[half(1 - c, i), pl.ds(first, n)], R0.at[:, pl.ds(at, n)], sibling)
            copies.append((copy, half(c, i), first, n, at))
        return copies

    def to_window(copies, at, n):
        for copy, mine_, first, size, to in copies:
            copy.wait_recv()
            R0[:, to : to + size] = R0[:, to : to + size] + C[mine_, first : first + size]
        return [
            go(R0.at[sixteen(16 * ((rho + dq) % 4)), pl.ds(at, n)], R1.at[t, :, pl.ds(at, n)], device)
            for t, (dq, device) in enumerate(steps)
        ]

    def add_window(copies, blocks):
        for copy in copies:
            copy.wait_recv()
        for i, first, n, at in blocks:
            for k in range(0, n, ROWS):
                cut = slice(at + k, at + k + ROWS)
                y_ = (y, yu, yd, yo)[(first + k) // ROWS]
                S1[i * 16 : (i + 1) * 16, pl.ds(pl.multiple_of(y_ * ROWS, ROWS), ROWS)] = (
                    R0[sixteen(16 * rho), cut] + R1[0, :, cut] + (R1[1, :, cut] + R1[2, :, cut])
                )

    early = [(0, 0, 384, 0), (1, 0, 384, 384), (2, 0, 384, 768)]
    rest = [(0, 384, 128, 1152), (1, 384, 128, 1280), (2, 384, 128, 1408), (3, 0, 512, 1536)]

    n_r1.wait_recv()
    flip(2, two)
    n_l1.wait_recv()
    flip(1, one)
    cross(0, 3, 0, y)
    d_u1.wait_recv()
    d_d1.wait_recv()
    send_b("y", y, "d", yd, *B)
    cross(0, 3, 1, yu)
    cross(0, 3, 2, yd)
    early_core = to_core(early)
    early_window = to_window(early_core, 0, 1152)
    hear(7)
    hear(8)
    tell(9, *(dev(dz=d) for d in hops))
    d_uo.wait_recv()
    d_do.wait_recv()
    cross(0, 3, 3, yo)
    n_ro.wait_recv()
    flip(3, one)
    n_lo.wait_recv()
    flip(3, two)
    C[3 * ROWS :, :] = jnp.dot(
        Nr[3 * ROWS :, :],
        jnp.concatenate([D[rows(x, y_)] for y_ in (y, yu, yd, yo)], axis=1),
        preferred_element_type=jnp.float32,
    )
    rest_core = to_core(rest)
    turn_a(A[0])
    add_window(early_window, early)
    rest_window = to_window(rest_core, 1152, 896)
    add_window(rest_window, rest)
    stride = [
        go(S1.at[sixteen(16 * (((z + d) % 16) // 4))], R2.at[k], dev(dz=d)) for k, d in enumerate(hops)
    ]
    turn_a(A[1])
    ao_r = go(blk(xl, y, 0, A_DEEP // 2), blk(xl, y, 0, A_DEEP // 2), right)
    ao_l = go(blk(xr, y, A_DEEP // 2, A_DEEP // 2), blk(xr, y, A_DEEP // 2, A_DEEP // 2), left)
    hear(9, 4)
    for copy in stride:
        copy.wait_recv()
    F[...] = ((R2[0] + R2[1]) + (R2[2] + R2[3])) * SCALE

    mine = sixteen(c * h + 16 * rho)

    def part(x_, at=None):
        return M.at[mine if at is None else at, pl.ds(pl.multiple_of(x_ * 512, 512), 512)]

    kept = sixteen(c * h + 16 * (z % 4))
    home = [go(F, part(x, kept), dev(dx=offset_of(s), dz=d)) for d in hops]

    fwd_a("r", xr, A[0])
    fwd_a("l", xl, A[0])
    send_b("u", yu, "o", yo, *B)
    fwd_b("y", y, "d", yd, *B)
    spread, pair = {}, []
    for k in (2, 3, 0, 1):
        home[k].wait_recv()
        region = part((x + 4 - offset_of(((z + 16 - hops[k]) % 16) // 4)) % 4)
        for t, (_, device) in enumerate(steps):
            spread[k, t] = go(region, region, device)
        pair.append(go(region, region, sibling))

    send_b("d", yd, "y", y, B[0])
    ao_r.wait_recv()
    ao_l.wait_recv()
    send_a("o", xo, AO[0])
    fwd_a("r", xr, A[1])

    for t, dq in ((0, 3), (1, 1), (2, 2)):
        for k in range(4):
            spread[k, t].wait_recv()
        region = M.at[sixteen(c * h + 16 * ((rho + dq) % 4))]
        pair.append(go(region, region, sibling))
    for copy in pair:
        copy.wait_recv()

    def between(step):
        if step == 0:
            send_a("o", xo, AO[1])
            send_b("d", yd, "y", y, *B[1:])
        if step == 1:
            send_a("o", xo, AO[2])
            send_b("o", yo, "u", yu, *B[:2])
        if step == 2:
            fwd_a("l", xl, A[1])
            fwd_a("o", xo, AO[0])
            send_b("o", yo, "u", yu, B[2])
            fwd_b("u", yu, "o", yo, B[0])
        if step == 3:
            fwd_a("o", xo, AO[1])
            fwd_a("o", xo, AO[2])
            fwd_b("u", yu, "o", yo, *B[1:])

    def block(k):
        return M[:, k * ROWS : (k + 1) * ROWS]

    def row_lse():
        top = block(0) + pbuf[0:1, :]
        for k in range(1, 16):
            top = jnp.maximum(top, block(k) + pbuf[k : k + 1, :])
        top = jnp.max(top, axis=1, keepdims=True)
        total = jnp.exp(block(0) + pbuf[0:1, :] - top)
        for k in range(1, 16):
            total = total + jnp.exp(block(k) + pbuf[k : k + 1, :] - top)
        return top + jnp.log(jnp.sum(total, axis=1, keepdims=True))

    near = [(dy, dx, 0, 0) for dy in range(4) for dx in range(4) if (dy, dx) != (0, 0)]
    near.sort(key=lambda peer: -min(peer[0], 4 - peer[0]) - min(peer[1], 4 - peer[1]))
    pbuf[...] = jnp.zeros_like(pbuf)
    for step in range(ITERS):
        rowpot = LOGA - row_lse()
        for k in range(16):
            values = block(k) + rowpot
            top = jnp.max(values, axis=0, keepdims=True)
            total = jnp.sum(jnp.exp(values - top), axis=0, keepdims=True)
            lbuf[step, k : k + 1, :] = top + jnp.log(total)
        slot = pl.ds(pl.multiple_of(b * 16, 16), 16)
        L[step, slot] = lbuf[step]
        swaps = [go(lbuf.at[step], L.at[step, slot], dev(*peer)) for peer in near]
        between(step)
        for copy in swaps:
            copy.wait_recv()
        top = L[step, 0:16]
        for k in range(1, 16):
            top = jnp.maximum(top, L[step, k * 16 : (k + 1) * 16])
        total = jnp.exp(L[step, 0:16] - top)
        for k in range(1, 16):
            total = total + jnp.exp(L[step, k * 16 : (k + 1) * 16] - top)
        pbuf[...] = LOGA - (top + jnp.log(total))

    lse = row_lse()
    for k in range(16):
        W[:, k * ROWS : (k + 1) * ROWS] = jnp.exp(block(k) + pbuf[k : k + 1, :] - lse).astype(jnp.bfloat16)
        pot_ref[(k % 4) * 4 + k // 4 : (k % 4) * 4 + k // 4 + 1, :] = pbuf[k : k + 1, :] * EPS

    for copy in [*b_r.values(), *b_l.values(), *late]:
        copy.wait_recv()
    for at in range(0, WIDE, TILE):
        all_rows = jnp.concatenate([D[k * DEEP + at : k * DEEP + at + TILE, :] for k in range(16)], axis=1)
        out_ref[at : at + TILE, :] = lax.dot_general(
            all_rows, W[...], (((1,), (1,)), ((), ())), preferred_element_type=jnp.float32
        ).astype(jnp.bfloat16)

    for copy in started:
        copy.wait_send()


def local(noise, data):
    f32, bf16 = jnp.float32, jnp.bfloat16
    vmem = pl.BlockSpec(memory_space=pltpu.VMEM)
    targets, potential = pl.pallas_call(
        kernel,
        name="pairing",
        out_shape=(jax.ShapeDtypeStruct((WIDE, ROWS), bf16), jax.ShapeDtypeStruct((16, ROWS), f32)),
        in_specs=[pl.BlockSpec(memory_space=pltpu.HBM)] * 2,
        out_specs=(vmem, vmem),
        scratch_shapes=[
            pltpu.VMEM((16 * DEEP, ROWS), bf16),
            pltpu.VMEM((4 * DEEP, ROWS), bf16),
            pltpu.VMEM((4 * ROWS, DEEP), bf16),
            pltpu.VMEM((512, 512), f32),
            pltpu.VMEM((64, 2048), f32),
            pltpu.VMEM((3, 16, 2048), f32),
            pltpu.VMEM((64, 512), f32),
            pltpu.VMEM((4, 16, 512), f32),
            pltpu.VMEM((16, 512), f32),
            pltpu.VMEM((ROWS, BATCH), f32),
            pltpu.VMEM((ITERS, 256, 128), f32),
            pltpu.VMEM((ITERS, 16, 128), f32),
            pltpu.VMEM((16, 128), f32),
            pltpu.VMEM((ROWS, BATCH), bf16),
            pltpu.SemaphoreType.REGULAR((10,)),
            pltpu.SemaphoreType.DMA((2,)),
            pltpu.SemaphoreType.DMA((N_SEM,)),
            pltpu.SemaphoreType.DMA((N_SEM,)),
        ],
        compiler_params=pltpu.CompilerParams(
            collective_id=0, has_side_effects=True, vmem_limit_bytes=48 * 1024 * 1024
        ),
    )(noise.T, data.T)
    return targets.T, potential.reshape(BATCH)


def solution(mesh):
    in_specs = (P("batch", "group"), P("batch", "group"))
    out_specs = (P("batch", "group"), P())
    return jax.shard_map(local, mesh=mesh, in_specs=in_specs, out_specs=out_specs, check_vma=False)
```

```python
import jax
import jax.numpy as jnp
import numpy as np
from jax import lax
from jax.experimental import pallas as pl
from jax.experimental.pallas import tpu as pltpu
from jax.sharding import PartitionSpec as P

MESH = pl.DeviceIdType.MESH
ITERS = 4
FEAT = 99840
BATCH = 2048
ROWS = 128
WIDE = 3120
DEEP = WIDE + 16
EPS = np.float32(2.0 / np.sqrt(np.float32(FEAT)))
LOGA = np.float32(-np.log(np.float32(BATCH)))
SCALE = np.float32(2.0 / (np.float64(FEAT) * np.float64(EPS)))
A = ((0, 784), (784, 1168))
AO = ((0, 656), (656, 656), (1312, 640))
A_DEEP = 1952
B = ((1952, 400), (2352, 400), (2752, 384))
HALF = 1536
N_SEM = 224
TILE = 624


def split3(value):
    high = value.astype(jnp.bfloat16).astype(jnp.float32)
    rest = value - high
    mid = rest.astype(jnp.bfloat16).astype(jnp.float32)
    return high, mid, rest - mid


def offset_of(s):
    return s + (s // 2) * (1 - 2 * (s % 2))


def place(dst, start, factor, own_at, const, const_at):
    def chunk(k, total):
        at = pl.multiple_of(k * 240, 16)
        piece = dst[pl.ds(pl.multiple_of(start + at, 16), 240)].astype(jnp.float32)
        return total + jnp.sum((piece * piece).reshape(30, 8, ROWS), axis=0)

    total = lax.fori_loop(0, WIDE // 240, chunk, jnp.zeros((8, ROWS), jnp.float32))
    parts = split3(jnp.sum(total, axis=0, keepdims=True) * factor)
    line = lax.broadcasted_iota(jnp.int32, (16, ROWS), 0)
    extra = jnp.zeros((16, ROWS), jnp.float32)
    for k, part in enumerate(parts):
        extra = jnp.where(line == own_at + k, part, extra)
        extra = jnp.where(line == const_at + k, jnp.float32(const), extra)
    dst[pl.ds(pl.multiple_of(start + WIDE, 16), 16)] = extra.astype(jnp.bfloat16)


def kernel(
    noise_ref, data_ref, out_ref, pot_ref,
    D, NT, Nr, C, R0, R1, S1, R2, F, M, L, lbuf, pbuf, W, known, load, send, recv,
):
    b = lax.axis_index("batch")
    g = lax.axis_index("group")
    y, x, z, c = b // 4, b % 4, g // 2, g % 2
    rho, s = (z + 2) % 4, z // 4
    hops = (6, 10, 2, 14)

    def dev(dy=0, dx=0, dz=0, dc=0):
        return (((y + dy) % 4) * 4 + (x + dx) % 4, ((z + dz) % 16) * 2 + (c + dc) % 2)

    right, left, up, down, sibling = dev(dx=1), dev(dx=3), dev(dy=1), dev(dy=3), dev(dc=1)
    count = [0]
    started = []

    def make(src, dst, device):
        k = count[0]
        count[0] += 1
        assert k < N_SEM
        return pltpu.make_async_remote_copy(src, dst, send.at[k], recv.at[k], device_id=device, device_id_type=MESH)

    def go(src, dst, device):
        copy = make(src, dst, device)
        copy.start()
        started.append(copy)
        return copy

    own = (x * 4 + y) * DEEP
    loads = [
        pltpu.make_async_copy(noise_ref, NT.at[pl.ds(0, WIDE)], load.at[0]),
        pltpu.make_async_copy(data_ref, D.at[pl.ds(pl.multiple_of(own, 16), WIDE)], load.at[1]),
    ]
    for copy in loads:
        copy.start()

    barrier = pltpu.get_barrier_semaphore()
    next_ones = (right, left, up, down, dev(dz=1), dev(dz=15), sibling)
    for device in next_ones:
        pl.semaphore_signal(barrier, inc=1, device_id=device, device_id_type=MESH)

    def tell(k, *devices):
        for device in devices:
            pl.semaphore_signal(known.at[k], inc=1, device_id=device, device_id_type=MESH)

    def hear(k, n=1):
        pl.semaphore_wait(known.at[k], n)

    def rows(x_, y_, first=0, n=DEEP):
        return pl.ds(pl.multiple_of((x_ * 4 + y_) * DEEP + first, 16), n)

    def blk(x_, y_, first=0, n=DEEP):
        return D.at[rows(x_, y_, first, n)]

    def nb(i, first, n):
        return NT.at[pl.ds(i * DEEP + first, n)]

    loads[0].wait()
    place(NT, 0, -0.5, 0, -0.5, 3)
    loads[1].wait()
    place(D, own, 1.0, 3, 1.0, 0)
    pl.semaphore_wait(barrier, len(next_ones))

    one, two = (0, HALF), (HALF, DEEP - HALF)
    n_r0 = go(nb(0, *one), nb(2, *one), right)
    n_l0 = go(nb(0, *two), nb(1, *two), left)
    d_u0 = go(blk(x, y, *one), blk(x, y, *one), up)
    d_d0 = go(blk(x, y, *two), blk(x, y, *two), down)
    n_r1 = go(nb(0, *two), nb(2, *two), right)
    n_l1 = go(nb(0, *one), nb(1, *one), left)
    d_u1 = go(blk(x, y, *two), blk(x, y, *two), up)
    d_d1 = go(blk(x, y, *one), blk(x, y, *one), down)
    xr, xl, xo = (x + 1) % 4, (x + 3) % 4, (x + 2) % 4
    yu, yd, yo = (y + 1) % 4, (y + 3) % 4, (y + 2) % 4
    tell(0, right)
    tell(1, up)
    tell(2, dev(dz=1))
    tell(3, dev(dz=15))

    def flip(i, part):
        first, n = part
        for at in range(first, first + n, ROWS):
            size = min(ROWS, first + n - at)
            Nr[i * ROWS : (i + 1) * ROWS, at : at + size] = NT[i * DEEP + at : i * DEEP + at + size, :].T

    flip(0, (0, DEEP))
    for k in range(4):
        hear(k)
    tell(4, dev(dz=2))
    tell(5, dev(dz=14))
    tell(6, up, down, dev(dy=2))
    n_r0.wait_recv()
    n_ro = go(nb(2, *one), nb(3, *one), right)
    n_l0.wait_recv()
    n_lo = go(nb(1, *two), nb(3, *two), left)
    d_u0.wait_recv()
    d_uo = go(blk(x, yd, *one), blk(x, yd, *one), up)
    d_d0.wait_recv()
    d_do = go(blk(x, yu, *two), blk(x, yu, *two), down)
    flip(2, one)
    flip(1, two)
    hear(4)
    hear(5)
    hear(6, 3)
    tell(7, dev(dz=2))
    tell(8, dev(dz=14))

    a_r, a_l = {}, {}
    for piece in A:
        a_r[piece] = go(blk(x, y, *piece), blk(x, y, *piece), right)
        a_l[piece] = go(blk(x, y, *piece), blk(x, y, *piece), left)
    b_r, b_l = {}, {}

    def send_b(r_name, r_y, l_name, l_y, *pieces):
        for piece in pieces:
            b_r[r_name, piece] = go(blk(x, r_y, *piece), blk(x, r_y, *piece), right)
            b_l[l_name, piece] = go(blk(x, l_y, *piece), blk(x, l_y, *piece), left)

    a_u, a_d = {}, {}

    def send_a(name, x_, piece):
        a_u[name, piece] = go(blk(x_, y, *piece), blk(x_, y, *piece), up)
        a_d[name, piece] = go(blk(x_, y, *piece), blk(x_, y, *piece), down)

    def turn_a(piece):
        a_r[piece].wait_recv()
        a_l[piece].wait_recv()
        send_a("r", xr, piece)
        send_a("l", xl, piece)

    late = []

    def fwd_b(r_name, r_y, l_name, l_y, *pieces):
        for piece in pieces:
            b_r.pop((r_name, piece)).wait_recv()
            late.append(go(blk(xl, r_y, *piece), blk(xl, r_y, *piece), right))
            b_l.pop((l_name, piece)).wait_recv()
            late.append(go(blk(xr, l_y, *piece), blk(xr, l_y, *piece), left))

    def fwd_a(name, x_, piece):
        first, size = piece
        n = size // 32 * 16
        a_u[name, piece].wait_recv()
        late.append(go(blk(x_, yd, first, n), blk(x_, yd, first, n), up))
        a_d[name, piece].wait_recv()
        late.append(go(blk(x_, yu, first + n, size - n), blk(x_, yu, first + n, size - n), down))

    def cross(i, n, j, y_):
        C[i * ROWS : (i + n) * ROWS, j * ROWS : (j + 1) * ROWS] = jnp.dot(
            Nr[i * ROWS : (i + n) * ROWS, :], D[rows(x, y_)], preferred_element_type=jnp.float32
        )

    h = ROWS // 2

    def half(core, i):
        return pl.ds(pl.multiple_of(i * ROWS + core * h, h), h)

    def sixteen(at):
        return pl.ds(pl.multiple_of(at, 16), 16)

    steps = [(1, dev(dz=1)), (3, dev(dz=15)), (2, dev(dz=18 - 4 * c))]

    def to_core(blocks):
        copies = []
        for i, first, n, at in blocks:
            copy = go(C.at[half(1 - c, i), pl.ds(first, n)], R0.at[:, pl.ds(at, n)], sibling)
            copies.append((copy, half(c, i), first, n, at))
        return copies

    def to_window(copies, at, n):
        for copy, mine_, first, size, to in copies:
            copy.wait_recv()
            R0[:, to : to + size] = R0[:, to : to + size] + C[mine_, first : first + size]
        return [
            go(R0.at[sixteen(16 * ((rho + dq) % 4)), pl.ds(at, n)], R1.at[t, :, pl.ds(at, n)], device)
            for t, (dq, device) in enumerate(steps)
        ]

    def add_window(copies, blocks):
        for copy in copies:
            copy.wait_recv()
        for i, first, n, at in blocks:
            for k in range(0, n, ROWS):
                cut = slice(at + k, at + k + ROWS)
                y_ = (y, yu, yd, yo)[(first + k) // ROWS]
                S1[i * 16 : (i + 1) * 16, pl.ds(pl.multiple_of(y_ * ROWS, ROWS), ROWS)] = (
                    R0[sixteen(16 * rho), cut] + R1[0, :, cut] + (R1[1, :, cut] + R1[2, :, cut])
                )

    early = [(0, 0, 384, 0), (1, 0, 384, 384), (2, 0, 384, 768)]
    rest = [(0, 384, 128, 1152), (1, 384, 128, 1280), (2, 384, 128, 1408), (3, 0, 512, 1536)]

    n_r1.wait_recv()
    flip(2, two)
    n_l1.wait_recv()
    flip(1, one)
    cross(0, 3, 0, y)
    d_u1.wait_recv()
    d_d1.wait_recv()
    send_b("y", y, "d", yd, *B[:2])
    cross(0, 3, 1, yu)
    cross(0, 3, 2, yd)
    early_core = to_core(early)
    early_window = to_window(early_core, 0, 1152)
    hear(7)
    hear(8)
    tell(9, *(dev(dz=d) for d in hops))
    d_uo.wait_recv()
    d_do.wait_recv()
    cross(0, 3, 3, yo)
    n_ro.wait_recv()
    flip(3, one)
    n_lo.wait_recv()
    flip(3, two)
    C[3 * ROWS :, :] = jnp.dot(
        Nr[3 * ROWS :, :],
        jnp.concatenate([D[rows(x, y_)] for y_ in (y, yu, yd, yo)], axis=1),
        preferred_element_type=jnp.float32,
    )
    rest_core = to_core(rest)
    turn_a(A[0])
    add_window(early_window, early)
    rest_window = to_window(rest_core, 1152, 896)
    add_window(rest_window, rest)
    stride = [
        go(S1.at[sixteen(16 * (((z + d) % 16) // 4))], R2.at[k], dev(dz=d)) for k, d in enumerate(hops)
    ]
    turn_a(A[1])
    ao_r = go(blk(xl, y, 0, A_DEEP // 2), blk(xl, y, 0, A_DEEP // 2), right)
    ao_l = go(blk(xr, y, A_DEEP // 2, A_DEEP // 2), blk(xr, y, A_DEEP // 2, A_DEEP // 2), left)
    send_b("y", y, "d", yd, B[2])
    hear(9, 4)
    for copy in stride:
        copy.wait_recv()
    F[...] = ((R2[0] + R2[1]) + (R2[2] + R2[3])) * SCALE

    mine = sixteen(c * h + 16 * rho)

    def part(x_, at=None):
        return M.at[mine if at is None else at, pl.ds(pl.multiple_of(x_ * 512, 512), 512)]

    kept = sixteen(c * h + 16 * (z % 4))
    home = [go(F, part(x, kept), dev(dx=offset_of(s), dz=d)) for d in hops]

    fwd_a("r", xr, A[0])
    fwd_a("l", xl, A[0])
    send_b("u", yu, "o", yo, *B)
    fwd_b("y", y, "d", yd, *B)
    spread, pair = {}, []
    for k in (2, 3, 0, 1):
        home[k].wait_recv()
        region = part((x + 4 - offset_of(((z + 16 - hops[k]) % 16) // 4)) % 4)
        for t, (_, device) in enumerate(steps):
            spread[k, t] = go(region, region, device)
        pair.append(go(region, region, sibling))

    send_b("d", yd, "y", y, B[0])
    ao_r.wait_recv()
    ao_l.wait_recv()
    send_a("o", xo, AO[0])
    fwd_a("r", xr, A[1])

    for t, dq in ((0, 3), (1, 1), (2, 2)):
        for k in range(4):
            spread[k, t].wait_recv()
        region = M.at[sixteen(c * h + 16 * ((rho + dq) % 4))]
        pair.append(go(region, region, sibling))
    for copy in pair:
        copy.wait_recv()

    def between(step):
        if step == 0:
            send_a("o", xo, AO[1])
            send_b("d", yd, "y", y, *B[1:])
        if step == 1:
            send_a("o", xo, AO[2])
            send_b("o", yo, "u", yu, *B[:2])
        if step == 2:
            fwd_a("l", xl, A[1])
            fwd_a("o", xo, AO[0])
            send_b("o", yo, "u", yu, B[2])
            fwd_b("u", yu, "o", yo, B[0])
        if step == 3:
            fwd_a("o", xo, AO[1])
            fwd_a("o", xo, AO[2])
            fwd_b("u", yu, "o", yo, *B[1:])

    def block(k):
        return M[:, k * ROWS : (k + 1) * ROWS]

    def row_lse():
        top = block(0) + pbuf[0:1, :]
        for k in range(1, 16):
            top = jnp.maximum(top, block(k) + pbuf[k : k + 1, :])
        top = jnp.max(top, axis=1, keepdims=True)
        total = jnp.exp(block(0) + pbuf[0:1, :] - top)
        for k in range(1, 16):
            total = total + jnp.exp(block(k) + pbuf[k : k + 1, :] - top)
        return top + jnp.log(jnp.sum(total, axis=1, keepdims=True))

    near = [(dy, dx, 0, 0) for dy in range(4) for dx in range(4) if (dy, dx) != (0, 0)]
    near.sort(key=lambda peer: -min(peer[0], 4 - peer[0]) - min(peer[1], 4 - peer[1]))
    pbuf[...] = jnp.zeros_like(pbuf)
    for step in range(ITERS):
        rowpot = LOGA - row_lse()
        for k in range(16):
            values = block(k) + rowpot
            top = jnp.max(values, axis=0, keepdims=True)
            total = jnp.sum(jnp.exp(values - top), axis=0, keepdims=True)
            lbuf[step, k : k + 1, :] = top + jnp.log(total)
        slot = pl.ds(pl.multiple_of(b * 16, 16), 16)
        L[step, slot] = lbuf[step]
        swaps = [go(lbuf.at[step], L.at[step, slot], dev(*peer)) for peer in near]
        between(step)
        for copy in swaps:
            copy.wait_recv()
        top = L[step, 0:16]
        for k in range(1, 16):
            top = jnp.maximum(top, L[step, k * 16 : (k + 1) * 16])
        total = jnp.exp(L[step, 0:16] - top)
        for k in range(1, 16):
            total = total + jnp.exp(L[step, k * 16 : (k + 1) * 16] - top)
        pbuf[...] = LOGA - (top + jnp.log(total))

    lse = row_lse()
    for k in range(16):
        W[:, k * ROWS : (k + 1) * ROWS] = jnp.exp(block(k) + pbuf[k : k + 1, :] - lse).astype(jnp.bfloat16)
        pot_ref[(k % 4) * 4 + k // 4 : (k % 4) * 4 + k // 4 + 1, :] = pbuf[k : k + 1, :] * EPS

    for copy in [*b_r.values(), *b_l.values(), *late]:
        copy.wait_recv()
    for at in range(0, WIDE, TILE):
        all_rows = jnp.concatenate([D[k * DEEP + at : k * DEEP + at + TILE, :] for k in range(16)], axis=1)
        out_ref[at : at + TILE, :] = lax.dot_general(
            all_rows, W[...], (((1,), (1,)), ((), ())), preferred_element_type=jnp.float32
        ).astype(jnp.bfloat16)

    for copy in started:
        copy.wait_send()


def local(noise, data):
    f32, bf16 = jnp.float32, jnp.bfloat16
    vmem = pl.BlockSpec(memory_space=pltpu.VMEM)
    targets, potential = pl.pallas_call(
        kernel,
        name="pairing",
        out_shape=(jax.ShapeDtypeStruct((WIDE, ROWS), bf16), jax.ShapeDtypeStruct((16, ROWS), f32)),
        in_specs=[pl.BlockSpec(memory_space=pltpu.HBM)] * 2,
        out_specs=(vmem, vmem),
        scratch_shapes=[
            pltpu.VMEM((16 * DEEP, ROWS), bf16),
            pltpu.VMEM((4 * DEEP, ROWS), bf16),
            pltpu.VMEM((4 * ROWS, DEEP), bf16),
            pltpu.VMEM((512, 512), f32),
            pltpu.VMEM((64, 2048), f32),
            pltpu.VMEM((3, 16, 2048), f32),
            pltpu.VMEM((64, 512), f32),
            pltpu.VMEM((4, 16, 512), f32),
            pltpu.VMEM((16, 512), f32),
            pltpu.VMEM((ROWS, BATCH), f32),
            pltpu.VMEM((ITERS, 256, 128), f32),
            pltpu.VMEM((ITERS, 16, 128), f32),
            pltpu.VMEM((16, 128), f32),
            pltpu.VMEM((ROWS, BATCH), bf16),
            pltpu.SemaphoreType.REGULAR((10,)),
            pltpu.SemaphoreType.DMA((2,)),
            pltpu.SemaphoreType.DMA((N_SEM,)),
            pltpu.SemaphoreType.DMA((N_SEM,)),
        ],
        compiler_params=pltpu.CompilerParams(
            collective_id=0, has_side_effects=True, vmem_limit_bytes=48 * 1024 * 1024
        ),
    )(noise.T, data.T)
    return targets.T, potential.reshape(BATCH)


def solution(mesh):
    in_specs = (P("batch", "group"), P("batch", "group"))
    out_specs = (P("batch", "group"), P())
    return jax.shard_map(local, mesh=mesh, in_specs=in_specs, out_specs=out_specs, check_vma=False)
```
